32 devices in a mesh: dp: 4 (over z), tp: 8 (over y, x, core).
Axes of the slice: x: 2, y: 2, z: 4, core: 2. Of those that a mesh axis runs over, the one named last changes fastest.
Arguments:
- layer_input: bfloat16 [128, 7168], P(('dp', 'tp')), may hold values from -16 to 16
- query: bfloat16 [128, 64, 576], P(('dp', 'tp')), may hold values from -48 to 48
- cache: bfloat16 [128, 2048, 576], P(('dp', 'tp')), may hold values from -8 to 8
- lengths: int32 [128], P(('dp', 'tp')), may hold values from 2 to 2048, as said below
- counts: int32 [32], P(('dp', 'tp')), may hold values from 1 to 4, as said below
- value_weight: bfloat16 [64, 512, 128], P('tp'), may hold values from -0.25 to 0.25
- output_weight: bfloat16 [8192, 7168], P('tp'), may hold values from -0.0625 to 0.0625
- norm_gain: float32 [7168], replicated, may hold values from 0.1 to 1.9
- gate_weight: bfloat16 [7168, 9216], P(None, 'tp'), may hold values from -0.0625 to 0.0625
- up_weight: bfloat16 [7168, 9216], P(None, 'tp'), may hold values from -0.0625 to 0.0625
- down_weight: bfloat16 [9216, 7168], P('tp', 'dp'), may hold values from -0.0625 to 0.0625
Outputs:
- layer_output: bfloat16 [128, 7168], P(('dp', 'tp'))
The draws below stay inside these ranges and needn't reach their ends.
Inputs may be any that keep to these rules, and one draw needn't show every extreme that they name: `counts`: one device holds 4 live slots and another one. `lengths`: on every device some live slot has 2048 valid positions.
All inputs are finite; a program needn't handle non-finite values.
Results may differ from the reference program's by a relative error of at most 0.014.
Values may be sent and summed in bfloat16 or wider, within the bound.
A program may use at most 128 MiB of HBM per device.

```python
import math
import jax
import jax.numpy as jnp
from jax import lax

D = 7168
FF = 9216
H = 64
LAT = 512
ROPE = 64
HEAD = 128
CTX = 2048
ROWS = 4
OWNERS = 32
SLOTS = 128


def shared_counts(key):
    key = jax.random.fold_in(key, 501)
    first_key, second_key, third_key = jax.random.split(key, 3)
    counts = jax.random.randint(first_key, (OWNERS,), 1, ROWS + 1)
    fullest = jax.random.randint(second_key, (), 0, OWNERS)
    emptiest = (fullest + 1 + jax.random.randint(third_key, (), 0, OWNERS - 1)) % OWNERS
    return counts.at[fullest].set(ROWS).at[emptiest].set(1)


def shared_keys(key):
    key = jax.random.fold_in(key, 611)
    first_key, second_key = jax.random.split(key, 2)
    leading = jnp.clip(jax.random.normal(first_key, (SLOTS, 2, LAT + ROPE), jnp.float32), -4.0, 4.0)
    latent_part = (jnp.arange(LAT + ROPE) < LAT).astype(jnp.float32)
    offset = 0.6 * jnp.clip(jax.random.normal(second_key, (SLOTS, 1, LAT + ROPE), jnp.float32), -4.0, 4.0) * latent_part
    return (leading, offset)


def draw_counts(key, part):
    return shared_counts(key)


def draw_lengths(key, part):
    counts = shared_counts(key)
    key = jax.random.fold_in(key, 13)
    first_key, second_key = jax.random.split(key, 2)
    lengths = jax.random.randint(first_key, (SLOTS,), 2, CTX + 1)
    picks = jax.random.randint(second_key, (OWNERS,), 0, 65536) % counts
    longest = jnp.arange(OWNERS, dtype=jnp.int32) * ROWS + picks
    return lengths.at[longest].set(CTX)


def draw_cache(key, part):
    leading, offset = shared_keys(key)
    key = jax.random.fold_in(key, 17)
    first_key = jax.random.fold_in(key, 0)
    noise = jnp.clip(jax.random.normal(first_key, (SLOTS, CTX, LAT + ROPE), jnp.float32), -4.0, 4.0)
    noise = jnp.concatenate([leading, noise[:, 2:]], axis=1)
    return (noise + offset).astype(jnp.bfloat16)


def draw_query(key, part):
    key = jax.random.fold_in(key, 19)
    first_key = jax.random.fold_in(key, 0)
    drawn = jnp.clip(jax.random.normal(first_key, (SLOTS, H, LAT + ROPE), jnp.float32), -4.0, 4.0)
    return drawn.astype(jnp.bfloat16)


def draw_layer_input(key, part):
    key = jax.random.fold_in(key, 23)
    first_key, second_key = jax.random.split(key, 2)
    base = jnp.clip(jax.random.normal(first_key, (SLOTS, D), jnp.float32), -4.0, 4.0)
    scales = jnp.exp(jax.random.uniform(second_key, (SLOTS, 1), jnp.float32, math.log(0.3), math.log(3.0)))
    return (base * scales).astype(jnp.bfloat16)


def levels(stream_key, extent, cuts, smallest, largest):
    loudness = 1.0
    for dim, blocks in cuts:
        draws = jax.random.uniform(jax.random.fold_in(jax.random.fold_in(stream_key, 6), dim), (blocks,), jnp.float32, smallest / len(cuts), largest / len(cuts))
        loudness = loudness * jnp.repeat(jnp.exp(draws), extent[dim] // blocks).reshape((-1,) + (1,) * (len(extent) - 1 - dim))
    return loudness


def scatter_about(key, dims, spread, reach, cuts=(), kind=jnp.bfloat16):
    values = jax.random.normal(key, dims, jnp.float32) * spread
    if len(cuts) > 0:
        values = levels(key, dims, cuts, -0.22, 0.18) * values
    return jnp.clip(values, min=-reach, max=reach).astype(kind)


def setup_inputs(seed: int = 0) -> dict:
    arg_keys = jax.random.split(jax.random.key(seed), 12)
    return {
        "layer_input": draw_layer_input(jax.random.fold_in(arg_keys[11], 71), 0),
        "query": draw_query(jax.random.fold_in(arg_keys[11], 71), 0),
        "cache": draw_cache(jax.random.fold_in(arg_keys[11], 71), 0),
        "lengths": draw_lengths(jax.random.fold_in(arg_keys[11], 71), 0),
        "counts": draw_counts(jax.random.fold_in(arg_keys[11], 71), 0),
        "value_weight": scatter_about(arg_keys[5], (H, LAT, HEAD), LAT ** -0.5, 0.25, ((0, 8),)),
        "output_weight": scatter_about(arg_keys[6], (H * HEAD, D), (H * HEAD) ** -0.5, 0.0625, ((0, 8),)),
        "norm_gain": jnp.clip(1.0 + 0.18 * jax.random.normal(arg_keys[7], (D,), jnp.float32), 0.1, 1.9),
        "gate_weight": scatter_about(arg_keys[8], (D, FF), D ** -0.5, 0.0625, ((1, 8),)),
        "up_weight": scatter_about(arg_keys[9], (D, FF), D ** -0.5, 0.0625, ((1, 8),)),
        "down_weight": scatter_about(arg_keys[10], (FF, D), FF ** -0.5, 0.0625, ((0, 8), (1, 4))),
    }


score_scale = 1.0 / 192.0 ** 0.5
norm_eps = 1e-06

def attend_one(items):
    question, stored, valid = items
    positions = jnp.arange(CTX, dtype=jnp.int32)
    visible = positions[None, :] < valid
    scores = jnp.einsum('hc,tc->ht', question.astype(jnp.float32), stored.astype(jnp.float32)) * score_scale
    scores = jnp.where(visible, scores, jnp.float32(-1e+30))
    peak = lax.optimization_barrier(jnp.max(scores, axis=1, keepdims=True))
    raised = jnp.where(visible, jnp.exp(scores - peak), jnp.float32(0.0))
    attention = (raised / lax.optimization_barrier(jnp.sum(raised, axis=1, keepdims=True))).astype(jnp.bfloat16)
    latent = jnp.einsum('ht,ta->ha', attention.astype(jnp.float32), stored[:, :LAT].astype(jnp.float32))
    return latent.astype(jnp.bfloat16)

def normalize(residual, norm_gain):
    wide = residual.astype(jnp.float32)
    square_mean = lax.optimization_barrier(jnp.mean(wide * wide, axis=1, keepdims=True))
    return (wide * lax.rsqrt(square_mean + norm_eps) * norm_gain[None, :]).astype(jnp.bfloat16)

def reference(layer_input, query, cache, lengths, counts, value_weight, output_weight, norm_gain, gate_weight, up_weight, down_weight):
    latent = lax.map(attend_one, (query, cache, lengths))
    values = jnp.einsum('rha,had->rhd', latent.astype(jnp.float32), value_weight.astype(jnp.float32)).astype(jnp.bfloat16)
    attended = jnp.dot(values.reshape(values.shape[0], H * HEAD), output_weight, preferred_element_type=jnp.float32)
    residual = (layer_input.astype(jnp.float32) + attended).astype(jnp.bfloat16)
    normed = normalize(residual, norm_gain)
    gate = jnp.dot(normed, gate_weight, preferred_element_type=jnp.float32)
    upward = jnp.dot(normed, up_weight, preferred_element_type=jnp.float32)
    inner = (jax.nn.silu(gate) * upward).astype(jnp.bfloat16)
    feed = jnp.dot(inner, down_weight, preferred_element_type=jnp.float32)
    slot_index = jnp.arange(SLOTS, dtype=jnp.int32)
    live = slot_index % ROWS < counts[slot_index // ROWS]
    mixed = residual.astype(jnp.float32) + feed
    return jnp.where(live[:, None], mixed, jnp.float32(0.0)).astype(jnp.bfloat16)
```

```python
import functools
import math

import jax
import jax.numpy as jnp
import numpy as np
from jax import lax
from jax.experimental import pallas as pl
from jax.experimental.pallas import tpu as pltpu
from jax.sharding import PartitionSpec as P

score_scale = 1.0 / 192.0**0.5
norm_eps = 1e-06
MESH = pl.DeviceIdType.MESH
F32 = jnp.float32
BF16 = jnp.bfloat16


def row_moves(n, m, slots, heads):
    each = heads // n
    send = np.zeros((slots * heads, slots * heads), np.float32)
    for o in range(slots * heads):
        j, r, h = o // (slots * each), (o // each) % slots, o % each
        send[o, r * heads + j * each + h] = 1
    group = n * slots
    take = np.zeros((each * group, each * group), np.float32)
    for o in range(each * group):
        h, j, r = o // group, (o % group) // slots, o % slots
        take[o, (j * slots + r) * each + h] = 1
    turn = np.zeros((m * group, m * group), np.float32)
    for o in range(m * group):
        j, g, r = o // (m * slots), (o // slots) % m, o % slots
        turn[o, g * group + j * slots + r] = 1
    return [x.astype(jnp.bfloat16) for x in (send, take, turn)]


def kernel(
    n,
    m,
    blocks,
    lengths,
    counts,
    layer_input,
    query,
    cache,
    value_weight,
    output_weight,
    gain,
    gate_weight,
    up_weight,
    down_weight,
    send_move,
    take_move,
    turn_move,
    out,
    cache_v,
    value_v,
    wo_v,
    gate_v,
    up_v,
    down_v,
    lat,
    lat_send,
    lat_recv,
    flat,
    rs_send,
    rs_recv,
    rs_own,
    ag,
    acc_gate,
    acc_up,
    square,
    inner,
    fs_send,
    fs_recv,
    z_send,
    z_recv,
    cache_sem,
    one_sem,
    wo_sem,
    gate_sem,
    up_sem,
    send_sem,
    recv_sem,
    dp_send_sem,
    dp_recv_sem,
):
    i = lax.axis_index("dp")
    j = lax.axis_index("tp")
    slots, heads, _ = query.shape
    width = lat.shape[2]
    group = n * slots
    rows = rs_send.shape[1]
    cols = rs_send.shape[2]
    each = heads // n
    row_blocks = group // rows
    jf = lax.rem(j, blocks)
    jr = lax.div(j, blocks)

    def cache_copy(r):
        slot = lax.rem(r, 2)
        return pltpu.make_async_copy(cache.at[r], cache_v.at[slot], cache_sem.at[slot])

    def wo_copy(b):
        source = output_weight.at[:, pl.ds(pl.multiple_of(b * cols, 128), cols)]
        return pltpu.make_async_copy(source, wo_v.at[b], wo_sem.at[b])

    def gate_copy(b):
        source = gate_weight.at[pl.ds(pl.multiple_of(b * cols, 128), cols), :]
        return pltpu.make_async_copy(source, gate_v.at[b], gate_sem.at[b])

    def up_copy(b):
        source = up_weight.at[pl.ds(pl.multiple_of(b * cols, 128), cols), :]
        return pltpu.make_async_copy(source, up_v.at[b], up_sem.at[b])

    value_copy = pltpu.make_async_copy(value_weight, value_v, one_sem.at[0])
    down_copy = pltpu.make_async_copy(down_weight, down_v, one_sem.at[1])

    def tp_copy(phase, source, target, peer, mine):
        return pltpu.make_async_remote_copy(
            src_ref=source,
            dst_ref=target,
            send_sem=send_sem.at[phase, peer],
            recv_sem=recv_sem.at[phase, mine],
            device_id=(i, peer),
            device_id_type=MESH,
        )

    def dp_copy(phase, source, target, peer, mine):
        return pltpu.make_async_remote_copy(
            src_ref=source,
            dst_ref=target,
            send_sem=dp_send_sem.at[phase, peer],
            recv_sem=dp_recv_sem.at[phase, mine],
            device_id=(peer, j),
            device_id_type=MESH,
        )

    def loop(count, body, first=0):
        def step(t, carry):
            body(t)
            return carry

        lax.fori_loop(first, count, step, 0)

    cache_copy(0).start()
    cache_copy(1).start()
    value_copy.start()
    loop(blocks, lambda t: wo_copy(lax.rem(jf + 1 + t, blocks)).start())

    barrier = pltpu.get_barrier_semaphore()

    def greet_tp(d):
        pl.semaphore_signal(
            barrier, inc=1, device_id=(i, lax.rem(j + d, n)), device_id_type=MESH
        )

    def greet_dp(d):
        pl.semaphore_signal(
            barrier, inc=1, device_id=(lax.rem(i + d, m), j), device_id_type=MESH
        )

    loop(n, greet_tp, 1)
    loop(m, greet_dp, 1)

    def attend(r):
        slot = lax.rem(r, 2)
        cache_copy(r).wait()
        question = query[r]
        stored = cache_v[slot]
        scores = (
            lax.dot_general(
                question, stored, (((1,), (1,)), ((), ())), preferred_element_type=F32
            )
            * score_scale
        )
        visible = lax.broadcasted_iota(jnp.int32, scores.shape, 1) < lengths[r]
        scores = jnp.where(visible, scores, F32(-1e30))
        peak = jnp.max(scores, axis=1, keepdims=True)
        raised = jnp.where(visible, jnp.exp(scores - peak), F32(0.0))
        total = jnp.sum(raised, axis=1, keepdims=True)
        mixed = jnp.dot(raised.astype(BF16), stored[:, :width], preferred_element_type=F32)
        lat[r] = (mixed / total).astype(BF16)

        @pl.when(r + 2 < slots)
        def _():
            cache_copy(r + 2).start()

        @pl.when(r == 1)
        def _():
            loop(blocks, lambda b: gate_copy(b).start())
            loop(blocks, lambda b: up_copy(b).start())
            down_copy.start()

    loop(slots, attend)

    moved = jnp.dot(
        send_move[...], lat[...].reshape(slots * heads, width), preferred_element_type=F32
    )
    lat_send[...] = moved.reshape(n, slots * each, width).astype(BF16)
    pl.semaphore_wait(barrier, n - 1 + m - 1)

    def send_latent(d):
        peer = lax.rem(j + d, n)
        tp_copy(0, lat_send.at[peer], lat_recv.at[j], peer, j).start()

    loop(n, send_latent, 1)
    lat_recv[j] = lat_send[j]
    value_copy.wait()

    def wait_latent(d):
        peer = lax.rem(j + n - d, n)
        tp_copy(0, lat_send.at[peer], lat_recv.at[peer], peer, peer).wait_recv()

    loop(n, wait_latent, 1)

    arrived = lat_recv[...].astype(F32).reshape(group * each, width).astype(BF16)
    taken = jnp.dot(take_move[...], arrived, preferred_element_type=F32).astype(BF16)
    head = value_v.shape[2]
    for h in range(each):
        flat[:, h * head : (h + 1) * head] = jnp.dot(
            taken[h * group : (h + 1) * group], value_v[h], preferred_element_type=F32
        ).astype(BF16)

    def project(t):
        b = lax.rem(jf + 1 + t, blocks)
        wo_copy(b).wait()
        part = jnp.dot(flat[...], wo_v[b], preferred_element_type=F32)
        mine = layer_input[:, pl.ds(pl.multiple_of(b * cols, 128), cols)].astype(F32)
        row = lax.broadcasted_iota(jnp.int32, part.shape, 0)
        for r in range(slots):
            part = part + jnp.where(row == j * slots + r, mine[r : r + 1, :], F32(0.0))
        for k in range(row_blocks):
            peer = k * blocks + b
            piece = part[k * rows : (k + 1) * rows]

            @pl.when(peer == j)
            def _():
                rs_own[...] = piece

            @pl.when(peer != j)
            def _():
                rs_send[peer] = piece.astype(BF16)
                tp_copy(1, rs_send.at[peer], rs_recv.at[j], peer, j).start()

    loop(blocks, project)

    def add_part(d):
        peer = lax.rem(j + n - d, n)
        tp_copy(1, rs_send.at[peer], rs_recv.at[peer], peer, peer).wait_recv()
        rs_own[...] += rs_recv[peer].astype(F32)

    loop(n, add_part, 1)
    ag[j] = rs_own[...].astype(BF16)

    def send_residual(d):
        peer = lax.rem(j + d, n)
        tp_copy(2, ag.at[j], ag.at[j], peer, j).start()

    loop(n, send_residual, 1)
    acc_gate[...] = jnp.zeros_like(acc_gate)
    acc_up[...] = jnp.zeros_like(acc_up)
    square[...] = jnp.zeros_like(square)

    def wait_weights(b):
        gate_copy(b).wait()
        up_copy(b).wait()

    loop(blocks, wait_weights)

    def expand(d):
        peer = lax.rem(j + n - d, n)

        @pl.when(d > 0)
        def _():
            tp_copy(2, ag.at[peer], ag.at[peer], peer, peer).wait_recv()

        k = lax.div(peer, blocks)
        b = lax.rem(peer, blocks)
        wide = ag[peer].astype(F32)
        square[k] += jnp.sum(wide * wide, axis=1, keepdims=True)
        scaled = (wide * gain[b]).astype(BF16)
        acc_gate[k] += jnp.dot(scaled, gate_v[b], preferred_element_type=F32)
        acc_up[k] += jnp.dot(scaled, up_v[b], preferred_element_type=F32)

    loop(n, expand)

    for k in range(row_blocks):
        norm = lax.rsqrt(square[k] * (1.0 / (blocks * cols)) + norm_eps)
        gate = acc_gate[k] * norm
        upward = acc_up[k] * norm
        inner[i, k * rows : (k + 1) * rows, :] = (
            gate / (1.0 + jnp.exp(-gate)) * upward
        ).astype(BF16)

    def send_inner(d):
        peer = lax.rem(i + d, m)
        dp_copy(0, inner.at[i], inner.at[i], peer, i).start()

    def wait_inner(d):
        peer = lax.rem(i + m - d, m)
        dp_copy(0, inner.at[peer], inner.at[peer], peer, peer).wait_recv()

    loop(m, send_inner, 1)
    down_copy.wait()
    loop(m, wait_inner, 1)

    every = inner[...].reshape(m * group, inner.shape[2])
    turned = jnp.dot(turn_move[...], every, preferred_element_type=F32).astype(BF16)
    fed = jnp.dot(turned, down_v[...], preferred_element_type=F32)
    fs_send[...] = fed.reshape(n, m * slots, fed.shape[1]).astype(BF16)

    def send_feed(d):
        peer = lax.rem(j + d, n)
        tp_copy(3, fs_send.at[peer], fs_recv.at[j], peer, j).start()

    loop(n, send_feed, 1)

    def add_feed(d, total):
        peer = lax.rem(j + n - d, n)
        tp_copy(3, fs_send.at[peer], fs_recv.at[peer], peer, peer).wait_recv()
        return total + fs_recv[peer].astype(F32)

    total = lax.fori_loop(1, n, add_feed, fs_send[j].astype(F32))
    pieces = blocks // m
    for g in range(m):
        for c in range(pieces):
            z_send[g, c * slots : (c + 1) * slots, :] = total[
                g * slots : (g + 1) * slots, c * cols : (c + 1) * cols
            ]

    def send_z(d):
        peer = lax.rem(i + d, m)
        dp_copy(1, z_send.at[peer], z_recv.at[i], peer, i).start()

    def wait_z(d):
        peer = lax.rem(i + m - d, m)
        dp_copy(1, z_send.at[peer], z_recv.at[peer], peer, peer).wait_recv()

    loop(m, send_z, 1)
    z_recv[i] = z_send[i]
    pick_row = lax.broadcasted_iota(jnp.int32, (8, rows), 0)
    pick_col = lax.broadcasted_iota(jnp.int32, (8, rows), 1)
    pick = jnp.where(pick_col == pick_row + jf * slots, F32(1.0), F32(0.0)).astype(BF16)
    live = lax.broadcasted_iota(jnp.int32, (slots, cols), 0) < counts[0]
    residual = [
        jnp.dot(pick, ag[jr * blocks + b], preferred_element_type=F32)[:slots]
        for b in range(blocks)
    ]
    loop(m, wait_z, 1)
    for b in range(blocks):
        g, c = b // pieces, b % pieces
        mixed = residual[b] + z_recv[g, c * slots : (c + 1) * slots, :]
        out[:, b * cols : (b + 1) * cols] = jnp.where(live, mixed, F32(0.0)).astype(BF16)

    def drain(d):
        peer = lax.rem(j + d, n)
        tp_copy(0, lat_send.at[peer], lat_recv.at[peer], peer, peer).wait_send()
        tp_copy(1, rs_send.at[peer], rs_recv.at[peer], peer, peer).wait_send()
        tp_copy(2, ag.at[j], ag.at[peer], peer, peer).wait_send()
        tp_copy(3, fs_send.at[peer], fs_recv.at[peer], peer, peer).wait_send()

    def drain_dp(d):
        peer = lax.rem(i + d, m)
        dp_copy(0, inner.at[i], inner.at[peer], peer, peer).wait_send()
        dp_copy(1, z_send.at[peer], z_recv.at[peer], peer, peer).wait_send()

    loop(n, drain, 1)
    loop(m, drain_dp, 1)


def on_device(
    n,
    m,
    layer_input,
    query,
    cache,
    lengths,
    counts,
    value_weight,
    output_weight,
    norm_gain,
    gate_weight,
    up_weight,
    down_weight,
):
    slots, features = layer_input.shape
    heads = query.shape[1]
    each, width, head = value_weight.shape
    hidden = gate_weight.shape[1]
    group = n * slots
    blocks = math.gcd(n, features // 128)
    cols = features // blocks
    rows = group * blocks // n
    part = down_weight.shape[1]
    moves = row_moves(n, m, slots, heads)
    vmem = pl.BlockSpec(memory_space=pltpu.VMEM)
    smem = pl.BlockSpec(memory_space=pltpu.SMEM)
    hbm = pl.BlockSpec(memory_space=pl.ANY)
    dma = pltpu.SemaphoreType.DMA
    return pl.pallas_call(
        functools.partial(kernel, n, m, blocks),
        out_shape=jax.ShapeDtypeStruct((slots, features), BF16),
        in_specs=[smem, smem, vmem, vmem, hbm, hbm, hbm, vmem, hbm, hbm, hbm, vmem, vmem, vmem],
        out_specs=vmem,
        scratch_shapes=[
            pltpu.VMEM((2,) + cache.shape[1:], BF16),
            pltpu.VMEM(value_weight.shape, BF16),
            pltpu.VMEM((blocks, each * head, cols), BF16),
            pltpu.VMEM((blocks, cols, hidden), BF16),
            pltpu.VMEM((blocks, cols, hidden), BF16),
            pltpu.VMEM(down_weight.shape, BF16),
            pltpu.VMEM((slots, heads, width), BF16),
            pltpu.VMEM((n, slots * each, width), BF16),
            pltpu.VMEM((n, slots * each, width), BF16),
            pltpu.VMEM((group, each * head), BF16),
            pltpu.VMEM((n, rows, cols), BF16),
            pltpu.VMEM((n, rows, cols), BF16),
            pltpu.VMEM((rows, cols), F32),
            pltpu.VMEM((n, rows, cols), BF16),
            pltpu.VMEM((group // rows, rows, hidden), F32),
            pltpu.VMEM((group // rows, rows, hidden), F32),
            pltpu.VMEM((group // rows, rows, 1), F32),
            pltpu.VMEM((m, group, hidden), BF16),
            pltpu.VMEM((n, m * slots, part), BF16),
            pltpu.VMEM((n, m * slots, part), BF16),
            pltpu.VMEM((m, slots * blocks // m, cols), F32),
            pltpu.VMEM((m, slots * blocks // m, cols), F32),
            dma((2,)),
            dma((2,)),
            dma((blocks,)),
            dma((blocks,)),
            dma((blocks,)),
            dma((4, n)),
            dma((4, n)),
            dma((2, m)),
            dma((2, m)),
        ],
        compiler_params=pltpu.CompilerParams(
            collective_id=0, has_side_effects=True, vmem_limit_bytes=64 * 1024 * 1024
        ),
    )(
        lengths,
        counts,
        layer_input,
        query,
        cache,
        value_weight,
        output_weight,
        norm_gain.reshape(blocks, 1, cols),
        gate_weight,
        up_weight,
        down_weight,
        *[jnp.asarray(x) for x in moves],
    )


def solution(mesh):
    placed = (
        P(("dp", "tp"), None),
        P(("dp", "tp"), None, None),
        P(("dp", "tp"), None, None),
        P(("dp", "tp")),
        P(("dp", "tp")),
        P("tp", None, None),
        P("tp", None),
        P(),
        P(None, "tp"),
        P(None, "tp"),
        P("tp", "dp"),
    )
    return jax.shard_map(
        functools.partial(on_device, mesh.shape["tp"], mesh.shape["dp"]),
        mesh=mesh,
        in_specs=placed,
        out_specs=P(("dp", "tp"), None),
        check_vma=False,
    )
```

```python
import functools
import math

import jax
import jax.numpy as jnp
import numpy as np
from jax import lax
from jax.experimental import pallas as pl
from jax.experimental.pallas import tpu as pltpu
from jax.sharding import PartitionSpec as P

score_scale = 1.0 / 192.0**0.5
norm_eps = 1e-06
MESH = pl.DeviceIdType.MESH
F32 = jnp.float32
BF16 = jnp.bfloat16


def row_moves(n, m, slots, heads):
    each, half = heads // n, slots // 2
    group = n * slots
    send = np.zeros((half * heads, half * heads), np.float32)
    for o in range(half * heads):
        j, r, h = o // (half * each), (o // each) % half, o % each
        send[o, r * heads + j * each + h] = 1
    take = np.zeros((2, each * group, half * heads), np.float32)
    for o in range(each * group):
        h, j, r = o // group, (o % group) // slots, o % slots
        take[r // half, o, (j * half + r % half) * each + h] = 1
    turn = np.zeros((m * group, m * group), np.float32)
    for o in range(m * group):
        j, g, r = o // (m * slots), (o // slots) % m, o % slots
        turn[o, g * group + j * slots + r] = 1
    return [x.astype(jnp.bfloat16) for x in (send, take, turn)]


def hidden_parts(hidden):
    if hidden % 128 or hidden < 512:
        return ((0, hidden),)
    first = (hidden // 2 + 127) // 128 * 128
    return ((0, first), (first, hidden))


def hidden_chunks(hidden):
    return tuple(
        tuple((at, min(at + 512, hi)) for at in range(lo, hi, 512)) for lo, hi in hidden_parts(hidden)
    )


def kernel(
    n,
    m,
    blocks,
    lengths,
    counts,
    layer_input,
    query,
    cache,
    value_weight,
    output_weight,
    gain,
    gate_weight,
    up_weight,
    down_weight,
    send_move,
    take_move,
    turn_move,
    out,
    cache_v,
    value_v,
    wo_v,
    gate_v,
    up_v,
    lat,
    lat_send,
    lat_recv,
    flat,
    rs_send,
    rs_recv,
    rs_own,
    ag,
    acc_gate,
    acc_up,
    square,
    inner,
    fs_recv,
    z_wide,
    z_send,
    z_recv,
    cache_sem,
    one_sem,
    wo_sem,
    gate_sem,
    up_sem,
    send_sem,
    recv_sem,
    dp_send_sem,
    dp_recv_sem,
):
    i = lax.axis_index("dp")
    j = lax.axis_index("tp")
    slots, heads, _ = query.shape
    half = slots // 2
    width = lat.shape[2]
    group = n * slots
    rows = rs_send.shape[1]
    cols = rs_send.shape[2]
    each = heads // n
    row_blocks = group // rows
    chips = n // 2
    pairs = blocks // 2
    wide_cols = 2 * cols
    parts = hidden_parts(gate_weight.shape[1])
    jf = lax.rem(j, blocks)
    jr = lax.div(j, blocks)
    core = lax.rem(j, 2)
    chip = lax.div(j, 2)
    sibling = chip * 2 + 1 - core
    ring = cache_v.shape[0]

    def cache_copy(r):
        slot = r % ring
        return pltpu.make_async_copy(cache.at[r], cache_v.at[slot], cache_sem.at[slot])

    def wo_copy(b):
        source = output_weight.at[:, pl.ds(pl.multiple_of(b * wide_cols, 128), wide_cols)]
        return pltpu.make_async_copy(source, wo_v.at[b], wo_sem.at[b])

    def gate_copy(b):
        source = gate_weight.at[pl.ds(pl.multiple_of(b * wide_cols, 128), wide_cols), :]
        return pltpu.make_async_copy(source, gate_v.at[b], gate_sem.at[b])

    def up_copy(b):
        source = up_weight.at[pl.ds(pl.multiple_of(b * wide_cols, 128), wide_cols), :]
        return pltpu.make_async_copy(source, up_v.at[b], up_sem.at[b])

    value_copy = pltpu.make_async_copy(value_weight, value_v, one_sem.at[0])
    chunks = hidden_chunks(gate_weight.shape[1])
    features = down_weight.shape[1]
    places = {c: k for k, c in enumerate(c for chunk in chunks for c in chunk)}

    def down_view(chunk):
        return cache_v.at[places[chunk], pl.ds(0, chunk[1] - chunk[0]), pl.ds(0, features)]

    def down_copy(chunk):
        source = down_weight.at[pl.ds(chunk[0], chunk[1] - chunk[0]), :]
        return pltpu.make_async_copy(source, down_view(chunk), one_sem.at[1 + places[chunk]])


    def tp_copy(phase, source, target, peer, mine):
        return pltpu.make_async_remote_copy(
            src_ref=source,
            dst_ref=target,
            send_sem=send_sem.at[phase, peer],
            recv_sem=recv_sem.at[phase, mine],
            device_id=(i, peer),
            device_id_type=MESH,
        )

    def dp_copy(phase, source, target, peer, mine):
        return pltpu.make_async_remote_copy(
            src_ref=source,
            dst_ref=target,
            send_sem=dp_send_sem.at[phase, peer],
            recv_sem=dp_recv_sem.at[phase, mine],
            device_id=(peer, j),
            device_id_type=MESH,
        )

    def loop(count, body, first=0):
        def step(t, carry):
            body(t)
            return carry

        lax.fori_loop(first, count, step, 0)

    for r in range(ring):
        cache_copy(r).start()
    value_copy.start()
    loop(pairs, lambda t: wo_copy(lax.rem(chip + 1 + t, pairs)).start())

    barrier = pltpu.get_barrier_semaphore()

    def greet_tp(d):
        pl.semaphore_signal(
            barrier, inc=1, device_id=(i, lax.rem(j + d, n)), device_id_type=MESH
        )

    def greet_dp(d):
        pl.semaphore_signal(
            barrier, inc=1, device_id=(lax.rem(i + d, m), j), device_id_type=MESH
        )

    loop(n, greet_tp, 1)
    loop(m, greet_dp, 1)

    def score(r):
        cache_copy(r).wait()
        return jnp.dot(query[r], cache_v[r % ring], preferred_element_type=F32) * score_scale

    def attend(r, scores):
        visible = lax.broadcasted_iota(jnp.int32, scores.shape, 1) < lengths[r]
        scores = jnp.where(visible, scores, F32(-1e30))
        peak = jnp.max(scores, axis=1, keepdims=True)
        raised = jnp.where(visible, jnp.exp(scores - peak), F32(0.0))
        total = jnp.sum(raised, axis=1, keepdims=True)
        mixed = lax.dot_general(
            raised.astype(BF16),
            cache_v[r % ring, :width, :],
            (((1,), (1,)), ((), ())),
            preferred_element_type=F32,
        )
        lat[r] = (mixed / total).astype(BF16)

    def send_latents(p):
        found = lat[p * half : (p + 1) * half].reshape(half * heads, width)
        moved = jnp.dot(send_move[...], found, preferred_element_type=F32)
        lat_send[p] = moved.reshape(n, half * each, width).astype(BF16)

        def send_latent(d):
            peer = lax.rem(j + d, n)
            tp_copy(p, lat_send.at[p, peer], lat_recv.at[p, j], peer, j).start()

        loop(n, send_latent, 1)
        lat_recv[p, j] = lat_send[p, j]

    ahead = score(0)
    for r in range(slots):
        scores = ahead
        if r + 1 < slots:
            ahead = score(r + 1)
        attend(r, scores)
        if r + ring < slots:
            cache_copy(r + ring).start()
        if r == 0:
            loop(pairs, lambda b: gate_copy(b).start())
            loop(pairs, lambda b: up_copy(b).start())
        if r == slots - 2:
            for chunk in places:
                down_copy(chunk).start()
        if r == half - 1:
            pl.semaphore_wait(barrier, n - 1 + m - 1)
            send_latents(0)
    send_latents(1)
    value_copy.wait()

    taken = jnp.zeros((each * group, width), F32)
    for p in range(2):

        def wait_latent(d):
            peer = lax.rem(j + n - d, n)
            tp_copy(p, lat_send.at[p, peer], lat_recv.at[p, peer], peer, peer).wait_recv()

        loop(n, wait_latent, 1)
        arrived = lat_recv[p].astype(F32).reshape(n * half * each, width).astype(BF16)
        taken = taken + jnp.dot(take_move[p], arrived, preferred_element_type=F32)
    taken = taken.astype(BF16)
    head = value_v.shape[2]
    for h in range(each):
        flat[:, h * head : (h + 1) * head] = jnp.dot(
            taken[h * group : (h + 1) * group], value_v[h], preferred_element_type=F32
        ).astype(BF16)

    def project(t):
        q = lax.rem(chip + 1 + t, pairs)
        wo_copy(q).wait()
        part = jnp.dot(flat[...], wo_v[q], preferred_element_type=F32)
        mine = layer_input[:, pl.ds(pl.multiple_of(q * wide_cols, 128), wide_cols)].astype(F32)
        row = lax.broadcasted_iota(jnp.int32, part.shape, 0)
        for r in range(slots):
            part = part + jnp.where(row == j * slots + r, mine[r : r + 1, :], F32(0.0))
        for k in range(row_blocks):
            for c in range(2):
                peer = k * blocks + q * 2 + c
                piece = part[k * rows : (k + 1) * rows, c * cols : (c + 1) * cols]

                @pl.when(peer == j)
                def _():
                    rs_own[...] = piece

                @pl.when(peer != j)
                def _():
                    rs_send[peer] = piece.astype(BF16)
                    tp_copy(2, rs_send.at[peer], rs_recv.at[j], peer, j).start()

    loop(pairs, project)

    def add_part(d):
        peer = lax.rem(j + n - d, n)
        tp_copy(2, rs_send.at[peer], rs_recv.at[peer], peer, peer).wait_recv()
        rs_own[...] += rs_recv[peer].astype(F32)

    loop(n, add_part, 1)
    ag[j] = rs_own[...].astype(BF16)

    tp_copy(3, ag.at[j], ag.at[j], sibling, j).start()

    def send_residual(d):
        peer = lax.rem(chip + d, chips) * 2 + core
        tp_copy(3, ag.at[j], ag.at[j], peer, j).start()

    loop(chips, send_residual, 1)
    acc_gate[...] = jnp.zeros_like(acc_gate)
    acc_up[...] = jnp.zeros_like(acc_up)
    square[...] = jnp.zeros_like(square)

    def wait_weights(b):
        gate_copy(b).wait()
        up_copy(b).wait()

    loop(pairs, wait_weights)

    def hand_on(source):
        return pltpu.make_async_remote_copy(
            src_ref=ag.at[source],
            dst_ref=ag.at[source],
            send_sem=send_sem.at[4, source],
            recv_sem=recv_sem.at[3, source],
            device_id=(i, sibling),
            device_id_type=MESH,
        )

    def expand(first, lo, hi, t):
        q = lax.rem(chip + chips - t, chips)
        if first:

            @pl.when(t + 1 < chips)
            def _():
                later = lax.rem(chip + chips - t - 1, chips) * 2 + core
                tp_copy(3, ag.at[later], ag.at[later], later, later).wait_recv()
                hand_on(later).start()

            other = q * 2 + 1 - core
            tp_copy(3, ag.at[other], ag.at[other], sibling, other).wait_recv()
        k = lax.div(q, pairs)
        b = lax.rem(q, pairs)
        wide = jnp.concatenate([ag[q * 2], ag[q * 2 + 1]], axis=1).astype(F32)
        if first:
            square[k] += jnp.sum(wide * wide, axis=1, keepdims=True)
        scaled = (wide * gain[b]).astype(BF16)
        acc_gate[k, :, lo:hi] += jnp.dot(scaled, gate_v[b, :, lo:hi], preferred_element_type=F32)
        acc_up[k, :, lo:hi] += jnp.dot(scaled, up_v[b, :, lo:hi], preferred_element_type=F32)

    for p, (lo, hi) in enumerate(parts):
        loop(chips, functools.partial(expand, p == 0, lo, hi))
        for k in range(row_blocks):
            norm = lax.rsqrt(square[k] * (1.0 / (blocks * cols)) + norm_eps)
            gate = acc_gate[k, :, lo:hi] * norm
            upward = acc_up[k, :, lo:hi] * norm
            inner[p][i, k * rows : (k + 1) * rows, :] = (
                gate / (1.0 + jnp.exp(-gate)) * upward
            ).astype(BF16)

        def send_inner(d):
            peer = lax.rem(i + d, m)
            dp_copy(p, inner[p].at[i], inner[p].at[i], peer, i).start()

        loop(m, send_inner, 1)

    fs_send = rs_send
    share = m * slots

    def drain_parts(d):
        peer = lax.rem(j + d, n)
        tp_copy(2, rs_send.at[peer], rs_recv.at[peer], peer, peer).wait_send()

    for chunk in places:
        down_copy(chunk).wait()
    pieces = blocks // m
    fed = [jnp.zeros((m * group, cols), F32) for _ in range(pieces)]
    for p, (lo, hi) in enumerate(parts):

        def wait_inner(d):
            peer = lax.rem(i + m - d, m)
            dp_copy(p, inner[p].at[peer], inner[p].at[peer], peer, peer).wait_recv()

        loop(m, wait_inner, 1)
        every = inner[p][...].reshape(m * group, hi - lo)
        turned = jnp.dot(turn_move[...], every, preferred_element_type=F32).astype(BF16)
        for c in range(pieces):
            for at, end in chunks[p]:
                fed[c] = fed[c] + jnp.dot(
                    turned[:, at - lo : end - lo],
                    cache_v[places[at, end], : end - at, c * cols : (c + 1) * cols],
                    preferred_element_type=F32,
                )
            if p == len(parts) - 1:
                if c == 0:
                    loop(n, drain_parts, 1)
                fs_send[:, c * share : (c + 1) * share, :] = (
                    fed[c].reshape(n, share, cols).astype(BF16)
                )

                def send_feed(d):
                    peer = lax.rem(j + d, n)
                    tp_copy(5 + c, fs_send.at[peer, pl.ds(c * share, share)], fs_recv.at[c, j], peer, j).start()

                loop(n, send_feed, 1)

    pick_row = lax.broadcasted_iota(jnp.int32, (8, rows), 0)
    pick_col = lax.broadcasted_iota(jnp.int32, (8, rows), 1)
    pick = jnp.where(pick_col == pick_row + jf * slots, F32(1.0), F32(0.0)).astype(BF16)
    live = lax.broadcasted_iota(jnp.int32, (slots, cols), 0) < counts[0]

    lanes = z_send.shape[3]
    for c in range(pieces):

        def add_feed(d, total):
            peer = lax.rem(j + n - d, n)
            tp_copy(5 + c, fs_send.at[peer, pl.ds(c * share, share)], fs_recv.at[c, peer], peer, peer).wait_recv()
            return total + fs_recv[c, peer].astype(F32)

        total = lax.fori_loop(1, n, add_feed, fs_send[j, c * share : (c + 1) * share].astype(F32))
        for g in range(m):
            for e, at in enumerate(range(0, cols, lanes)):
                span = min(lanes, cols - at)
                z_wide[g, e * slots : (e + 1) * slots, :span] = total[
                    g * slots : (g + 1) * slots, at : at + span
                ]
        z_send[c] = z_wide[...].astype(BF16)

        def send_z(d):
            peer = lax.rem(i + d, m)
            dp_copy(2 + c, z_send.at[c, peer], z_recv.at[c, i], peer, i).start()

        loop(m, send_z, 1)
        z_recv[c, i] = z_send[c, i]

    for c in range(pieces):

        def wait_z(d):
            peer = lax.rem(i + m - d, m)
            dp_copy(2 + c, z_send.at[c, peer], z_recv.at[c, peer], peer, peer).wait_recv()

        loop(m, wait_z, 1)
        for g in range(m):
            b = g * pieces + c
            residual = jnp.dot(pick, ag[jr * blocks + b], preferred_element_type=F32)
            summed = z_recv[c, g].astype(F32)
            for e, at in enumerate(range(0, cols, lanes)):
                span = min(lanes, cols - at)
                mixed = residual[:slots, at : at + span] + summed[
                    e * slots : (e + 1) * slots, :span
                ]
                out[:, b * cols + at : b * cols + at + span] = jnp.where(
                    live[:, :span], mixed, F32(0.0)
                ).astype(BF16)

    def drain(d):
        peer = lax.rem(j + d, n)
        for p in range(2):
            tp_copy(p, lat_send.at[p, peer], lat_recv.at[p, peer], peer, peer).wait_send()
        for c in range(pieces):
            tp_copy(5 + c, fs_send.at[peer, pl.ds(c * share, share)], fs_recv.at[c, peer], peer, peer).wait_send()

    def drain_residual(d):
        peer = lax.rem(chip + d, chips) * 2 + core
        tp_copy(3, ag.at[j], ag.at[j], peer, peer).wait_send()
        hand_on(peer).wait_send()

    def drain_dp(d):
        peer = lax.rem(i + d, m)
        for p in range(len(parts)):
            dp_copy(p, inner[p].at[i], inner[p].at[i], peer, peer).wait_send()
        for c in range(pieces):
            dp_copy(2 + c, z_send.at[c, peer], z_recv.at[c, peer], peer, peer).wait_send()

    loop(n, drain, 1)
    tp_copy(3, ag.at[j], ag.at[j], sibling, sibling).wait_send()
    loop(chips, drain_residual, 1)
    loop(m, drain_dp, 1)


def on_device(
    n,
    m,
    layer_input,
    query,
    cache,
    lengths,
    counts,
    value_weight,
    output_weight,
    norm_gain,
    gate_weight,
    up_weight,
    down_weight,
):
    slots, features = layer_input.shape
    heads = query.shape[1]
    each, width, head = value_weight.shape
    hidden = gate_weight.shape[1]
    group = n * slots
    blocks = math.gcd(n, features // 128)
    cols = features // blocks
    rows = group * blocks // n
    pieces = blocks // m
    lanes = (cols // 4 + 127) // 128 * 128
    cache = cache.transpose(0, 2, 1)
    moves = row_moves(n, m, slots, heads)
    vmem = pl.BlockSpec(memory_space=pltpu.VMEM)
    smem = pl.BlockSpec(memory_space=pltpu.SMEM)
    hbm = pl.BlockSpec(memory_space=pl.ANY)
    dma = pltpu.SemaphoreType.DMA
    return pl.pallas_call(
        functools.partial(kernel, n, m, blocks),
        out_shape=jax.ShapeDtypeStruct((slots, features), BF16),
        in_specs=[smem, smem, vmem, vmem, hbm, hbm, hbm, vmem, hbm, hbm, hbm, vmem, vmem, vmem],
        out_specs=vmem,
        scratch_shapes=[
            pltpu.VMEM(cache.shape, BF16),
            pltpu.VMEM(value_weight.shape, BF16),
            pltpu.VMEM((blocks // 2, each * head, 2 * cols), BF16),
            pltpu.VMEM((blocks // 2, 2 * cols, hidden), BF16),
            pltpu.VMEM((blocks // 2, 2 * cols, hidden), BF16),
            pltpu.VMEM((slots, heads, width), BF16),
            pltpu.VMEM((2, n, slots // 2 * each, width), BF16),
            pltpu.VMEM((2, n, slots // 2 * each, width), BF16),
            pltpu.VMEM((group, each * head), BF16),
            pltpu.VMEM((n, rows, cols), BF16),
            pltpu.VMEM((n, rows, cols), BF16),
            pltpu.VMEM((rows, cols), F32),
            pltpu.VMEM((n, rows, cols), BF16),
            pltpu.VMEM((group // rows, rows, hidden), F32),
            pltpu.VMEM((group // rows, rows, hidden), F32),
            pltpu.VMEM((group // rows, rows, 1), F32),
            [pltpu.VMEM((m, group, hi - lo), BF16) for lo, hi in hidden_parts(hidden)],
            pltpu.VMEM((pieces, n, m * slots, cols), BF16),
            pltpu.VMEM((m, 4 * slots, lanes), F32),
            pltpu.VMEM((pieces, m, 4 * slots, lanes), BF16),
            pltpu.VMEM((pieces, m, 4 * slots, lanes), BF16),
            dma((slots,)),
            dma((slots,)),
            dma((blocks // 2,)),
            dma((blocks // 2,)),
            dma((blocks // 2,)),
            dma((5 + pieces, n)),
            dma((5 + pieces, n)),
            dma((2 + pieces, m)),
            dma((2 + pieces, m)),
        ],
        compiler_params=pltpu.CompilerParams(
            collective_id=0, has_side_effects=True, vmem_limit_bytes=64 * 1024 * 1024
        ),
    )(
        lengths,
        counts,
        layer_input,
        query,
        cache,
        value_weight,
        output_weight,
        norm_gain.reshape(blocks // 2, 1, 2 * cols),
        gate_weight,
        up_weight,
        down_weight,
        *[jnp.asarray(x) for x in moves],
    )


def solution(mesh):
    placed = (
        P(("dp", "tp"), None),
        P(("dp", "tp"), None, None),
        P(("dp", "tp"), None, None),
        P(("dp", "tp")),
        P(("dp", "tp")),
        P("tp", None, None),
        P("tp", None),
        P(),
        P(None, "tp"),
        P(None, "tp"),
        P("tp", "dp"),
    )
    return jax.shard_map(
        functools.partial(on_device, mesh.shape["tp"], mesh.shape["dp"]),
        mesh=mesh,
        in_specs=placed,
        out_specs=P(("dp", "tp"), None),
        check_vma=False,
    )
```

```python
import functools
import math

import jax
import jax.numpy as jnp
import numpy as np
from jax import lax
from jax.experimental import pallas as pl
from jax.experimental.pallas import tpu as pltpu
from jax.sharding import PartitionSpec as P

score_scale = 1.0 / 192.0**0.5
norm_eps = 1e-06
MESH = pl.DeviceIdType.MESH
F32 = jnp.float32
BF16 = jnp.bfloat16


def row_moves(n, m, slots, heads):
    each, half = heads // n, slots // 2
    group = n * slots
    send = np.zeros((half * heads, half * heads), np.float32)
    for o in range(half * heads):
        j, r, h = o // (half * each), (o // each) % half, o % each
        send[o, r * heads + j * each + h] = 1
    take = np.zeros((2, each * group, half * heads), np.float32)
    for o in range(each * group):
        h, j, r = o // group, (o % group) // slots, o % slots
        take[r // half, o, (j * half + r % half) * each + h] = 1
    turn = np.zeros((m * group, m * group), np.float32)
    for o in range(m * group):
        j, g, r = o // (m * slots), (o // slots) % m, o % slots
        turn[o, g * group + j * slots + r] = 1
    return [x.astype(jnp.bfloat16) for x in (send, take, turn)]


def hidden_parts(hidden):
    if hidden % 128 or hidden < 512:
        return ((0, hidden),)
    first = hidden * 4 // 9 // 128 * 128
    second = first + hidden // 3 // 128 * 128
    return ((0, first), (first, second), (second, hidden))


def hidden_chunks(hidden):
    return tuple(
        tuple((at, min(at + 512, hi)) for at in range(lo, hi, 512)) for lo, hi in hidden_parts(hidden)
    )


def kernel(
    n,
    m,
    blocks,
    lengths,
    counts,
    layer_input,
    query,
    cache,
    value_weight,
    output_weight,
    gain,
    gate_weight,
    up_weight,
    down_weight,
    send_move,
    take_move,
    turn_move,
    out,
    cache_v,
    value_v,
    wo_v,
    gate_v,
    up_v,
    lat,
    lat_send,
    lat_recv,
    flat,
    rs_send,
    rs_recv,
    rs_own,
    ag,
    acc_gate,
    acc_up,
    square,
    inner,
    rs_pair,
    fs_recv,
    z_wide,
    z_send,
    z_recv,
    cache_sem,
    one_sem,
    wo_sem,
    gate_sem,
    up_sem,
    send_sem,
    recv_sem,
    dp_send_sem,
    dp_recv_sem,
):
    i = lax.axis_index("dp")
    j = lax.axis_index("tp")
    slots, heads, _ = query.shape
    half = slots // 2
    width = lat.shape[2]
    group = n * slots
    rows = rs_send.shape[1]
    cols = rs_send.shape[2]
    each = heads // n
    row_blocks = group // rows
    chips = n // 2
    pairs = blocks // 2
    wide_cols = 2 * cols
    parts = hidden_parts(gate_weight.shape[1])
    jf = lax.rem(j, blocks)
    jr = lax.div(j, blocks)
    core = lax.rem(j, 2)
    chip = lax.div(j, 2)
    sibling = chip * 2 + 1 - core
    ring = cache_v.shape[0]

    def cache_copy(r):
        slot = r % ring
        return pltpu.make_async_copy(cache.at[r], cache_v.at[slot], cache_sem.at[slot])

    def wo_copy(b):
        source = output_weight.at[:, pl.ds(pl.multiple_of(b * wide_cols, 128), wide_cols)]
        return pltpu.make_async_copy(source, wo_v.at[b], wo_sem.at[b])

    def gate_copy(b):
        source = gate_weight.at[pl.ds(pl.multiple_of(b * wide_cols, 128), wide_cols), :]
        return pltpu.make_async_copy(source, gate_v.at[b], gate_sem.at[b])

    def up_copy(b):
        source = up_weight.at[pl.ds(pl.multiple_of(b * wide_cols, 128), wide_cols), :]
        return pltpu.make_async_copy(source, up_v.at[b], up_sem.at[b])

    value_copy = pltpu.make_async_copy(value_weight, value_v, one_sem.at[0])
    chunks = hidden_chunks(gate_weight.shape[1])
    features = down_weight.shape[1]
    places = {c: k for k, c in enumerate(c for chunk in chunks for c in chunk)}

    def down_view(chunk):
        return cache_v.at[places[chunk], pl.ds(0, chunk[1] - chunk[0]), pl.ds(0, features)]

    def down_copy(chunk):
        source = down_weight.at[pl.ds(chunk[0], chunk[1] - chunk[0]), :]
        return pltpu.make_async_copy(source, down_view(chunk), one_sem.at[1 + places[chunk]])


    def tp_copy(phase, source, target, peer, mine):
        return pltpu.make_async_remote_copy(
            src_ref=source,
            dst_ref=target,
            send_sem=send_sem.at[phase, peer],
            recv_sem=recv_sem.at[phase, mine],
            device_id=(i, peer),
            device_id_type=MESH,
        )

    def dp_copy(phase, source, target, peer, mine):
        return pltpu.make_async_remote_copy(
            src_ref=source,
            dst_ref=target,
            send_sem=dp_send_sem.at[phase, peer],
            recv_sem=dp_recv_sem.at[phase, mine],
            device_id=(peer, j),
            device_id_type=MESH,
        )

    def loop(count, body, first=0):
        def step(t, carry):
            body(t)
            return carry

        lax.fori_loop(first, count, step, 0)

    def start_wo(t):
        wo_copy(lax.rem(chip + 1 + t, pairs)).start()

    cache_copy(0).start()
    cache_copy(1).start()

    barrier = pltpu.get_barrier_semaphore()

    def greet_tp(d):
        pl.semaphore_signal(
            barrier, inc=1, device_id=(i, lax.rem(j + d, n)), device_id_type=MESH
        )

    def greet_dp(d):
        pl.semaphore_signal(
            barrier, inc=1, device_id=(lax.rem(i + d, m), j), device_id_type=MESH
        )

    loop(n, greet_tp, 1)
    loop(m, greet_dp, 1)

    def score(r):
        cache_copy(r).wait()
        if r == 0:
            for later in range(2, slots):
                cache_copy(later).start()
            value_copy.start()
            start_wo(0)
        return jnp.dot(query[r], cache_v[r % ring], preferred_element_type=F32) * score_scale

    def attend(r, scores):
        visible = lax.broadcasted_iota(jnp.int32, scores.shape, 1) < lengths[r]
        scores = jnp.where(visible, scores, F32(-1e30))
        peak = jnp.max(scores, axis=1, keepdims=True)
        raised = jnp.where(visible, jnp.exp(scores - peak), F32(0.0))
        total = jnp.sum(raised, axis=1, keepdims=True)
        mixed = lax.dot_general(
            raised.astype(BF16),
            cache_v[r % ring, :width, :],
            (((1,), (1,)), ((), ())),
            preferred_element_type=F32,
        )
        lat[r] = (mixed / total).astype(BF16)

    def send_latents(p):
        found = lat[p * half : (p + 1) * half].reshape(half * heads, width)
        moved = jnp.dot(send_move[...], found, preferred_element_type=F32)
        lat_send[p] = moved.reshape(n, half * each, width).astype(BF16)

        def send_latent(d):
            peer = lax.rem(j + d, n)
            tp_copy(p, lat_send.at[p, peer], lat_recv.at[p, j], peer, j).start()

        loop(n, send_latent, 1)
        lat_recv[p, j] = lat_send[p, j]

    def start_weights(t):
        b = lax.rem(chip + chips - t, pairs)
        gate_copy(b).start()
        up_copy(b).start()

    ahead = score(0)
    for r in range(slots):
        scores = ahead
        if r + 1 < slots:
            ahead = score(r + 1)
        attend(r, scores)
        if r == 0:
            loop(pairs, start_wo, 1)
        if r == 1:
            start_weights(0)
        if r == slots - 2:
            loop(pairs, start_weights, 1)
            for chunk in places:
                down_copy(chunk).start()
        if r == half - 1:
            pl.semaphore_wait(barrier, n - 1 + m - 1)
            send_latents(0)
    send_latents(1)
    value_copy.wait()

    taken = jnp.zeros((each * group, width), F32)
    for p in range(2):

        def wait_latent(d):
            peer = lax.rem(j + n - d, n)
            tp_copy(p, lat_send.at[p, peer], lat_recv.at[p, peer], peer, peer).wait_recv()

        loop(n, wait_latent, 1)
        arrived = lat_recv[p].astype(F32).reshape(n * half * each, width).astype(BF16)
        taken = taken + jnp.dot(take_move[p], arrived, preferred_element_type=F32)
    taken = taken.astype(BF16)
    head = value_v.shape[2]
    for h in range(each):
        flat[:, h * head : (h + 1) * head] = jnp.dot(
            taken[h * group : (h + 1) * group], value_v[h], preferred_element_type=F32
        ).astype(BF16)

    def project(t):
        q = lax.rem(chip + 1 + t, pairs)
        wo_copy(q).wait()
        part = jnp.dot(flat[...], wo_v[q], preferred_element_type=F32)
        mine = layer_input[:, pl.ds(pl.multiple_of(q * wide_cols, 128), wide_cols)].astype(F32)
        row = lax.broadcasted_iota(jnp.int32, part.shape, 0)
        for r in range(slots):
            part = part + jnp.where(row == j * slots + r, mine[r : r + 1, :], F32(0.0))
        for k in range(row_blocks):
            for c in range(2):
                peer = k * blocks + q * 2 + c
                piece = part[k * rows : (k + 1) * rows, c * cols : (c + 1) * cols]

                @pl.when(peer == j)
                def _():
                    rs_own[...] = piece

                @pl.when(peer != j)
                def _():
                    rs_send[peer] = piece.astype(BF16)
                    tp_copy(2, rs_send.at[peer], rs_recv.at[j], peer, j).start()

    loop(pairs, project)

    def add_part(d):
        peer = lax.rem(j + n - d, n)
        tp_copy(2, rs_send.at[peer], rs_recv.at[peer], peer, peer).wait_recv()
        rs_own[...] += rs_recv[peer].astype(F32)

    loop(n, add_part, 1)
    ag[j] = rs_own[...].astype(BF16)

    tp_copy(3, ag.at[j], ag.at[j], sibling, j).start()

    def send_residual(d):
        peer = lax.rem(chip + d, chips) * 2 + core
        tp_copy(3, ag.at[j], ag.at[j], peer, j).start()

    loop(chips, send_residual, 1)
    acc_gate[...] = jnp.zeros_like(acc_gate)
    acc_up[...] = jnp.zeros_like(acc_up)
    square[...] = jnp.zeros_like(square)

    def hand_on(source):
        return pltpu.make_async_remote_copy(
            src_ref=ag.at[source],
            dst_ref=ag.at[source],
            send_sem=send_sem.at[4, source],
            recv_sem=recv_sem.at[3, source],
            device_id=(i, sibling),
            device_id_type=MESH,
        )

    def expand(first, lo, hi, t):
        q = lax.rem(chip + chips - t, chips)
        if first:

            @pl.when(t + 1 < chips)
            def _():
                later = lax.rem(chip + chips - t - 1, chips) * 2 + core
                tp_copy(3, ag.at[later], ag.at[later], later, later).wait_recv()
                hand_on(later).start()

            other = q * 2 + 1 - core
            tp_copy(3, ag.at[other], ag.at[other], sibling, other).wait_recv()
        k = lax.div(q, pairs)
        b = lax.rem(q, pairs)
        if first:

            @pl.when(t < pairs)
            def _():
                gate_copy(b).wait()
                up_copy(b).wait()

        if first:
            wide = jnp.concatenate([ag[q * 2], ag[q * 2 + 1]], axis=1).astype(F32)
            square[k] += jnp.sum(wide * wide, axis=1, keepdims=True)
            scaled = (wide * gain[b]).astype(BF16)
            rs_recv[q * 2] = scaled[:, :cols]
            rs_recv[q * 2 + 1] = scaled[:, cols:]
        else:
            scaled = jnp.concatenate([rs_recv[q * 2], rs_recv[q * 2 + 1]], axis=1)
        acc_gate[k, :, lo:hi] += jnp.dot(scaled, gate_v[b, :, lo:hi], preferred_element_type=F32)
        acc_up[k, :, lo:hi] += jnp.dot(scaled, up_v[b, :, lo:hi], preferred_element_type=F32)

    for p, (lo, hi) in enumerate(parts):
        if p > 0 and chips <= 4:
            for t in range(chips):
                expand(False, lo, hi, t)
        else:
            loop(chips, functools.partial(expand, p == 0, lo, hi))
        for k in range(row_blocks):
            norm = lax.rsqrt(square[k] * (1.0 / (blocks * cols)) + norm_eps)
            gate = acc_gate[k, :, lo:hi] * norm
            upward = acc_up[k, :, lo:hi] * norm
            inner[p][i, k * rows : (k + 1) * rows, :] = (
                gate / (1.0 + jnp.exp(-gate)) * upward
            ).astype(BF16)

        def send_inner(d):
            peer = lax.rem(i + d, m)
            dp_copy(p, inner[p].at[i], inner[p].at[i], peer, i).start()

        loop(m, send_inner, 1)

    fs_send = rs_send
    share = m * slots

    def piece_of(c):
        return pl.ds(c * share, share)

    def pair_copy(c, q):
        return pltpu.make_async_remote_copy(
            src_ref=fs_send.at[q * 2 + 1 - core, piece_of(c)],
            dst_ref=rs_pair.at[q, piece_of(c)],
            send_sem=send_sem.at[5 + c, q],
            recv_sem=recv_sem.at[5 + c, q],
            device_id=(i, sibling),
            device_id_type=MESH,
        )

    def feed_copy(c, peer, origin):
        return tp_copy(
            5 + pieces + c, fs_send.at[peer, piece_of(c)], fs_recv.at[c, origin], peer, origin
        )

    def drain_parts(d):
        peer = lax.rem(j + d, n)
        tp_copy(2, rs_send.at[peer], rs_recv.at[peer], peer, peer).wait_send()

    for chunk in places:
        down_copy(chunk).wait()
    pieces = blocks // m
    fed = [jnp.zeros((m * group, cols), F32) for _ in range(pieces)]
    for p, (lo, hi) in enumerate(parts):

        def wait_inner(d):
            peer = lax.rem(i + m - d, m)
            dp_copy(p, inner[p].at[peer], inner[p].at[peer], peer, peer).wait_recv()

        loop(m, wait_inner, 1)
        every = inner[p][...].reshape(m * group, hi - lo)
        turned = jnp.dot(turn_move[...], every, preferred_element_type=F32).astype(BF16)
        for c in range(pieces):
            for at, end in chunks[p]:
                fed[c] = fed[c] + jnp.dot(
                    turned[:, at - lo : end - lo],
                    cache_v[places[at, end], : end - at, c * cols : (c + 1) * cols],
                    preferred_element_type=F32,
                )
            if p == len(parts) - 1:
                if c == 0:
                    loop(n, drain_parts, 1)
                fs_send[:, c * share : (c + 1) * share, :] = (
                    fed[c].reshape(n, share, cols).astype(BF16)
                )

                def send_pair(d):
                    q = lax.rem(chip + d, chips)
                    pair_copy(c, q).start()

                loop(chips + 1, send_pair, 1)

    for c in range(pieces):

        def send_feed(d):
            q = lax.rem(chip + d, chips)
            peer = q * 2 + core
            pair_copy(c, q).wait_recv()
            summed = fs_send[peer, c * share : (c + 1) * share].astype(F32) + rs_pair[
                q, c * share : (c + 1) * share
            ].astype(F32)
            fs_send[peer, c * share : (c + 1) * share] = summed.astype(BF16)
            feed_copy(c, peer, chip).start()

        loop(chips, send_feed, 1)

    pick_row = lax.broadcasted_iota(jnp.int32, (8, rows), 0)
    pick_col = lax.broadcasted_iota(jnp.int32, (8, rows), 1)
    pick = jnp.where(pick_col == pick_row + jf * slots, F32(1.0), F32(0.0)).astype(BF16)
    live = lax.broadcasted_iota(jnp.int32, (slots, cols), 0) < counts[0]

    lanes = z_send.shape[3]
    for c in range(pieces):

        def add_feed(d, total):
            q = lax.rem(chip + chips - d, chips)
            feed_copy(c, q * 2 + core, q).wait_recv()
            return total + fs_recv[c, q].astype(F32)

        pair_copy(c, chip).wait_recv()
        total = fs_send[j, c * share : (c + 1) * share].astype(F32) + rs_pair[
            chip, c * share : (c + 1) * share
        ].astype(F32)
        total = lax.fori_loop(1, chips, add_feed, total)
        for g in range(m):
            for e, at in enumerate(range(0, cols, lanes)):
                span = min(lanes, cols - at)
                z_wide[g, e * slots : (e + 1) * slots, :span] = total[
                    g * slots : (g + 1) * slots, at : at + span
                ]
        z_send[c] = z_wide[...].astype(BF16)

        def send_z(d):
            peer = lax.rem(i + d, m)
            dp_copy(len(parts) + c, z_send.at[c, peer], z_recv.at[c, i], peer, i).start()

        loop(m, send_z, 1)
        z_recv[c, i] = z_send[c, i]

    for c in range(pieces):

        def wait_z(d):
            peer = lax.rem(i + m - d, m)
            dp_copy(len(parts) + c, z_send.at[c, peer], z_recv.at[c, peer], peer, peer).wait_recv()

        loop(m, wait_z, 1)
        for g in range(m):
            b = g * pieces + c
            residual = jnp.dot(pick, ag[jr * blocks + b], preferred_element_type=F32)
            summed = z_recv[c, g].astype(F32)
            for e, at in enumerate(range(0, cols, lanes)):
                span = min(lanes, cols - at)
                mixed = residual[:slots, at : at + span] + summed[
                    e * slots : (e + 1) * slots, :span
                ]
                out[:, b * cols + at : b * cols + at + span] = jnp.where(
                    live[:, :span], mixed, F32(0.0)
                ).astype(BF16)

    def drain(d):
        peer = lax.rem(j + d, n)
        for p in range(2):
            tp_copy(p, lat_send.at[p, peer], lat_recv.at[p, peer], peer, peer).wait_send()

    def drain_residual(d):
        peer = lax.rem(chip + d, chips) * 2 + core
        tp_copy(3, ag.at[j], ag.at[j], peer, peer).wait_send()
        hand_on(peer).wait_send()
        for c in range(pieces):
            feed_copy(c, peer, chip).wait_send()

    def drain_pair(q):
        for c in range(pieces):
            pair_copy(c, q).wait_send()

    def drain_dp(d):
        peer = lax.rem(i + d, m)
        for p in range(len(parts)):
            dp_copy(p, inner[p].at[i], inner[p].at[i], peer, peer).wait_send()
        for c in range(pieces):
            dp_copy(len(parts) + c, z_send.at[c, peer], z_recv.at[c, peer], peer, peer).wait_send()

    loop(n, drain, 1)
    tp_copy(3, ag.at[j], ag.at[j], sibling, sibling).wait_send()
    loop(chips, drain_residual, 1)
    loop(chips, drain_pair)
    loop(m, drain_dp, 1)


def on_device(
    n,
    m,
    layer_input,
    query,
    cache,
    lengths,
    counts,
    value_weight,
    output_weight,
    norm_gain,
    gate_weight,
    up_weight,
    down_weight,
):
    slots, features = layer_input.shape
    heads = query.shape[1]
    each, width, head = value_weight.shape
    hidden = gate_weight.shape[1]
    group = n * slots
    blocks = math.gcd(n, features // 128)
    cols = features // blocks
    rows = group * blocks // n
    pieces = blocks // m
    lanes = (cols // 4 + 127) // 128 * 128
    cache = cache.transpose(0, 2, 1)
    moves = row_moves(n, m, slots, heads)
    vmem = pl.BlockSpec(memory_space=pltpu.VMEM)
    smem = pl.BlockSpec(memory_space=pltpu.SMEM)
    hbm = pl.BlockSpec(memory_space=pl.ANY)
    dma = pltpu.SemaphoreType.DMA
    return pl.pallas_call(
        functools.partial(kernel, n, m, blocks),
        out_shape=jax.ShapeDtypeStruct((slots, features), BF16),
        in_specs=[smem, smem, vmem, vmem, hbm, hbm, hbm, vmem, hbm, hbm, hbm, vmem, vmem, vmem],
        out_specs=vmem,
        scratch_shapes=[
            pltpu.VMEM(cache.shape, BF16),
            pltpu.VMEM(value_weight.shape, BF16),
            pltpu.VMEM((blocks // 2, each * head, 2 * cols), BF16),
            pltpu.VMEM((blocks // 2, 2 * cols, hidden), BF16),
            pltpu.VMEM((blocks // 2, 2 * cols, hidden), BF16),
            pltpu.VMEM((slots, heads, width), BF16),
            pltpu.VMEM((2, n, slots // 2 * each, width), BF16),
            pltpu.VMEM((2, n, slots // 2 * each, width), BF16),
            pltpu.VMEM((group, each * head), BF16),
            pltpu.VMEM((n, rows, cols), BF16),
            pltpu.VMEM((n, rows, cols), BF16),
            pltpu.VMEM((rows, cols), F32),
            pltpu.VMEM((n, rows, cols), BF16),
            pltpu.VMEM((group // rows, rows, hidden), F32),
            pltpu.VMEM((group // rows, rows, hidden), F32),
            pltpu.VMEM((group // rows, rows, 1), F32),
            [pltpu.VMEM((m, group, hi - lo), BF16) for lo, hi in hidden_parts(hidden)],
            pltpu.VMEM((n // 2, pieces * m * slots, cols), BF16),
            pltpu.VMEM((pieces, n // 2, m * slots, cols), BF16),
            pltpu.VMEM((m, 4 * slots, lanes), F32),
            pltpu.VMEM((pieces, m, 4 * slots, lanes), BF16),
            pltpu.VMEM((pieces, m, 4 * slots, lanes), BF16),
            dma((slots,)),
            dma((slots,)),
            dma((blocks // 2,)),
            dma((blocks // 2,)),
            dma((blocks // 2,)),
            dma((5 + 2 * pieces, n)),
            dma((5 + 2 * pieces, n)),
            dma((len(hidden_parts(hidden)) + pieces, m)),
            dma((len(hidden_parts(hidden)) + pieces, m)),
        ],
        compiler_params=pltpu.CompilerParams(
            collective_id=0, has_side_effects=True, vmem_limit_bytes=64 * 1024 * 1024
        ),
    )(
        lengths,
        counts,
        layer_input,
        query,
        cache,
        value_weight,
        output_weight,
        norm_gain.reshape(blocks // 2, 1, 2 * cols),
        gate_weight,
        up_weight,
        down_weight,
        *[jnp.asarray(x) for x in moves],
    )


def solution(mesh):
    placed = (
        P(("dp", "tp"), None),
        P(("dp", "tp"), None, None),
        P(("dp", "tp"), None, None),
        P(("dp", "tp")),
        P(("dp", "tp")),
        P("tp", None, None),
        P("tp", None),
        P(),
        P(None, "tp"),
        P(None, "tp"),
        P("tp", "dp"),
    )
    return jax.shard_map(
        functools.partial(on_device, mesh.shape["tp"], mesh.shape["dp"]),
        mesh=mesh,
        in_specs=placed,
        out_specs=P(("dp", "tp"), None),
        check_vma=False,
    )
```
